256 devices in a mesh: tok: 32 (over z, x), voc: 8 (over y, core).
Axes of the slice: x: 4, y: 4, z: 8, core: 2. Of those that a mesh axis runs over, the one named last changes fastest.
Arguments:
- hidden_states: bfloat16 [4096, 4096], P('tok', 'voc'), may hold values from -20 to 20
- head: bfloat16 [4096, 65536], P('voc', 'tok'), may hold values from -0.0625 to 0.0625
- proj_in: bfloat16 [4096, 128], P('voc'), may hold values from -0.09375 to 0.09375
- proj_out: bfloat16 [65536, 128], P('tok'), may hold values from -6 to 6
- targets: int32 [4096], P('voc'), may hold values from 0 to 65535
- lengths: int32 [8, 8], P('voc'), may hold values from 1 to 256, 512 in all within a row
Outputs:
- attributions: float32 [64, 128, 128], P('voc', 'tok')
The draws below stay inside these ranges and needn't reach their ends.
Inputs may be any that keep to these rules, and one draw needn't show every extreme that they name: The lengths of each sequence add up to 512.
All inputs are finite; a program needn't handle non-finite values.
Results may differ from the reference program's by a relative error of at most 0.0031.
Values may be sent and summed in bfloat16 or wider, within the bound.
No kernel may reach another device: no remote copies, remote signals or barrier semaphores. Data moves between devices by JAX's collectives and lax.ppermute only.
A program may use at most 128 MiB of HBM per device.

```python
import math
import jax
import jax.numpy as jnp
import numpy as np
from jax import lax

D = 4096
VOCAB = 65536
PIN = 128
POUT = 128
EX_SEQ = 8
TOKENS = 4096
SEQS = 8
SEQ = 512
EXAMPLES = 64
N_VOC = 8


def column_signs(key, cols):

    def one_column(col):
        return jax.random.rademacher(jax.random.fold_in(key, col), (D,), dtype=jnp.float32)
    return jax.vmap(one_column)(cols)


def draw_head(key, part):
    signs = column_signs(key, jnp.arange(VOCAB, dtype=jnp.int32))
    return (4.0 * D ** (-0.5) * signs.T).astype(jnp.bfloat16)


def planted_rows(key_plant, sign_key, values):
    key_column, key_strength = jax.random.split(key_plant, 2)
    rows = jnp.arange(TOKENS)
    chosen = jax.random.randint(key_column, (TOKENS,), 0, VOCAB - 1)
    strength = jax.random.uniform(key_strength, (TOKENS,), jnp.float32, 30.0, 70.0)
    strength = jnp.where(rows == 5, 70.0, strength)
    leading_amp = (strength * D ** (-0.5))[:, None]
    runner_amp = leading_amp - 0.5 * D ** (-0.5)
    leading = column_signs(sign_key, chosen)
    runner = column_signs(sign_key, chosen + 1)
    aligned = leading_amp * leading + runner_amp * runner
    picked = (rows % 37 == 5)[:, None]
    return jnp.where(picked, aligned, values)


def draw_hidden_states(key, part):
    sign_key = key
    key = jax.random.fold_in(key, 11)
    key_base = jax.random.fold_in(key, 0)
    key_plant = jax.random.fold_in(key, 2)
    base = jax.random.truncated_normal(key_base, -6.0, 6.0, (TOKENS, D), jnp.float32)
    values = base
    values = planted_rows(key_plant, sign_key, values)
    return jnp.clip(values, -20.0, 20.0).astype(jnp.bfloat16)


def place_ends(entries, own_key, low, top_value):
    spot = [jax.random.randint(jax.random.fold_in(own_key, axis), (), 0, length) for axis, length in enumerate(entries.shape)]
    widest = entries.shape.index(max(entries.shape))
    next_to = spot[:widest] + [(spot[widest] + 1) % entries.shape[widest]] + spot[widest + 1:]
    return entries.at[tuple(spot)].set(low).at[tuple(next_to)].set(top_value)


def level_of(own_key, dims, pieces, smallest, largest):
    def one(dim, blocks):
        draws = jax.random.uniform(jax.random.fold_in(jax.random.fold_in(own_key, 6), dim), (blocks,), jnp.float32, smallest / len(pieces), largest / len(pieces))
        return jnp.repeat(jnp.exp(draws), dims[dim] // blocks).reshape((-1,) + (1,) * (len(dims) - dim - 1))

    level = one(*pieces[0])
    for cut in pieces[1:]:
        level = level * one(*cut)
    return level


def rank_bounds(count, skew):
    portions = [(1 << 20) // math.isqrt(standing ** skew) + 1 for standing in range(1, count + 1)]
    deviation = 1 + sum(portions) // (1 << 30)
    return np.cumsum(np.array([max(1, weight // deviation) for weight in portions]))


def skewed_ids(rng, shape, amount, slope):
    table = rank_bounds(amount, slope)
    ticket = jax.random.randint(jax.random.fold_in(rng, 1), shape, 0, int(table[amount - 1]))
    grade = jnp.searchsorted(jnp.asarray(table, jnp.int32), ticket, side="right")
    return jax.random.permutation(jax.random.fold_in(rng, 2), amount)[grade].astype(jnp.int32)


def profile(number_of, total, limit, skew):
    portions = [(1 << 20) // math.isqrt(standing ** skew) + 1 for standing in range(2, number_of + 1)]
    rest, given = total - limit - (number_of - 1), [1] * (number_of - 1)
    while rest > 0:
        candidates = [i for i in range(number_of - 1) if given[i] < limit]
        mass, budget = sum([portions[i] for i in candidates]), rest
        for i in candidates:
            extra = min(limit - given[i], max(1, budget * portions[i] // mass), rest)
            given[i] = given[i] + extra
            rest = rest - extra
    return np.array([limit] + given)


def uneven_parts(key, count, total, bound, lean):
    if count == 2:
        one = jax.random.randint(key, (), max(1, total - bound), min(bound, total - 1) + 1)
        return jnp.stack([one, total - one])
    tallies = jnp.asarray(profile(count, total, bound, lean), jnp.int32)
    couples = (count - 1) // 2
    donor, sink = tallies[1:1 + 2 * couples:2], tallies[2:2 + 2 * couples:2]
    margin = jnp.minimum(donor - 1, bound - sink)
    moved = jax.random.randint(jax.random.fold_in(key, 1), (couples,), 0, 1 << 20) % (margin + 1)
    tallies = tallies.at[1:1 + 2 * couples:2].set(donor - moved).at[2:2 + 2 * couples:2].set(sink + moved)
    return tallies[jax.random.permutation(jax.random.fold_in(key, 2), count)]


def normal_values(stream_key, extent, scale, most, pieces=(), held_as=jnp.bfloat16):
    entries = scale * jax.random.normal(stream_key, extent, jnp.float32)
    if pieces:
        entries = entries * level_of(stream_key, extent, pieces, -0.22, 0.18)
    return jnp.clip(entries, -most, most).astype(held_as)


def setup_inputs(seed: int = 0) -> dict:
    streams_of = jax.random.split(jax.random.key(seed), 7)
    return {
        "hidden_states": draw_hidden_states(jax.random.fold_in(streams_of[6], 71), 0),
        "head": draw_head(jax.random.fold_in(streams_of[6], 71), 0),
        "proj_in": normal_values(streams_of[2], (D, PIN), D ** -0.5, 0.09375, ((0, 8),)),
        "proj_out": normal_values(streams_of[3], (VOCAB, POUT), 1.0, 6.0, ((0, 32),)),
        "targets": place_ends(skewed_ids(streams_of[4], (TOKENS,), VOCAB, 2), jax.random.fold_in(streams_of[4], 3), 0, VOCAB - 1).astype(jnp.int32),
        "lengths": jax.vmap(lambda own: uneven_parts(own, EX_SEQ, SEQ, SEQ // 2, 2))(jax.random.split(streams_of[5], SEQS)).reshape((SEQS, EX_SEQ)).astype(jnp.int32),
    }


def reference(hidden_states, head, proj_in, proj_out, targets, lengths):
    width = D // N_VOC

    def one_sequence(seq_index):
        first_row = (seq_index * SEQ).astype(jnp.int32)
        seq_rows = lax.dynamic_slice_in_dim(hidden_states, first_row, SEQ, 0)
        seq_targets = lax.dynamic_slice_in_dim(targets, first_row, SEQ, 0)
        seq_lengths = lax.dynamic_slice_in_dim(lengths, seq_index.astype(jnp.int32), 1, 0)[0]
        logits = jnp.zeros((SEQ, VOCAB), jnp.float32)
        in_sum = jnp.zeros((SEQ, PIN), jnp.float32)
        for slice_index in range(N_VOC):
            feature_piece = seq_rows[:, slice_index * width:(slice_index + 1) * width]
            head_piece = head[slice_index * width:(slice_index + 1) * width]
            in_piece = proj_in[slice_index * width:(slice_index + 1) * width]
            logits = logits + jnp.dot(feature_piece, head_piece, preferred_element_type=jnp.float32)
            in_sum = in_sum + jnp.dot(feature_piece, in_piece, preferred_element_type=jnp.float32)
        in_proj = in_sum.astype(jnp.bfloat16)
        row_max = jnp.max(logits, axis=1)
        shifted = jnp.exp(logits - row_max[:, None])
        row_total = jnp.sum(shifted, axis=1)
        columns = jnp.arange(VOCAB, dtype=jnp.int32)
        onehot = (seq_targets[:, None] == columns[None, :]).astype(jnp.float32)
        grad_logits = (shifted / row_total[:, None] - onehot).astype(jnp.bfloat16)
        out_proj = jnp.dot(grad_logits, proj_out, preferred_element_type=jnp.float32)
        ends = jnp.cumsum(seq_lengths).astype(jnp.int32)
        starts = ends - seq_lengths
        positions = jnp.arange(SEQ, dtype=jnp.int32)
        member = ((positions[:, None] >= starts[None, :]) & (positions[:, None] < ends[None, :])).astype(jnp.float32)
        membership = member / seq_lengths.astype(jnp.float32)[None, :]
        expanded = membership[:, :, None] * in_proj.astype(jnp.float32)[:, None, :]
        return jnp.einsum("ter,tc->erc", expanded, out_proj, precision=lax.Precision.HIGHEST)

    result = lax.map(one_sequence, jnp.arange(SEQS, dtype=jnp.int32))
    return result.reshape(EXAMPLES, PIN, POUT)
```

```python
import functools

import jax
import jax.numpy as jnp
from jax import lax
from jax.experimental import pallas as pl
from jax.experimental.pallas import tpu as pltpu
from jax.sharding import Mesh, PartitionSpec as P

TILE = 512
F32 = jnp.float32
BF16 = jnp.bfloat16


def shift(x, axis, by):
    n = lax.axis_size(axis)
    return lax.ppermute(x, axis, [(i, (i + by) % n) for i in range(n)])


def swap(x):
    return shift(x, "c", 1)


def exchange_corners(x):
    pairs = []
    for z in range(8):
        for xx in range(4):
            for v in range(8):
                src = (z * 4 + xx) * 8 + v
                dst = (v * 4 + xx) * 8 + z
                pairs.append((src, dst))
    return lax.ppermute(x, ("z", "x", "y", "c"), pairs)


def gather_hidden(block):
    z = lax.axis_index("z")
    x = lax.axis_index("x")
    mine = jnp.zeros((512, 512), BF16)
    for by in (0, 1, 3, 2):
        got = block if by == 0 else shift(block, "x", by)
        mine = lax.dynamic_update_slice(mine, got, (((x - by) % 4) * 128, 0))
    stack = jnp.zeros((8, 512, 512), BF16)

    def put(stack, piece, slot, row=0):
        return lax.dynamic_update_slice(stack, piece[None], (slot % 8, row, 0))

    stack = put(stack, mine, z)
    right, left = mine, mine
    for step in (1, 2, 3):
        right = shift(right, "z", 1)
        left = shift(left, "z", -1)
        stack = put(stack, right, z - step)
        stack = put(stack, left, z + step)
    far_a = shift(right[:256], "z", 1)
    far_b = shift(left[256:], "z", -1)
    stack = put(stack, far_a, z + 4, 0)
    return put(stack, far_b, z + 4, 256)


def dots(hid_ref, slot_ref, pieces, refs, acc):
    for ref, (place, low, rows) in zip(refs, pieces):
        acc_part = jnp.dot(
            hid_ref[slot_ref[place], :, low : low + rows], ref[...], preferred_element_type=F32
        )
        acc = acc_part if acc is None else acc + acc_part
    return acc


def first_kernel(pieces, slot_ref, hid_ref, pin_ref, *refs):
    heads, (part_ref, in_ref) = refs[: len(pieces)], refs[len(pieces) :]

    @pl.when(pl.program_id(0) == 0)
    def _():
        acc = jnp.dot(hid_ref[0], pin_ref[0], preferred_element_type=F32)
        for d in range(1, 8):
            acc = acc + jnp.dot(hid_ref[d], pin_ref[d], preferred_element_type=F32)
        in_ref[...] = acc.astype(BF16)

    part_ref[...] = dots(hid_ref, slot_ref, pieces, heads, None)


def last_kernel(pieces, slot_ref, hid_ref, part_ref, proj_ref, tgt_ref, *refs):
    heads, (out_ref, max_ref, rest_ref, hit_ref, sum_ref) = refs[: len(pieces)], refs[len(pieces) :]
    step = pl.program_id(0)

    @pl.when(step == 0)
    def _():
        max_ref[...] = jnp.full_like(max_ref, -jnp.inf)
        rest_ref[...] = jnp.zeros_like(rest_ref)
        hit_ref[...] = jnp.zeros_like(hit_ref)
        sum_ref[...] = jnp.zeros_like(sum_ref)

    logits = dots(hid_ref, slot_ref, pieces, heads, part_ref[...])
    old = max_ref[...]
    new = jnp.maximum(old, jnp.max(logits, axis=1, keepdims=True))
    scale = jnp.exp(old - new)
    shifted = jnp.exp(logits - new)
    columns = lax.broadcasted_iota(jnp.int32, logits.shape, 1) + step * TILE
    at_target = columns == tgt_ref[...]
    rest = jnp.where(at_target, 0.0, shifted)
    hit = jnp.where(at_target, shifted, 0.0)
    max_ref[...] = new
    rest_ref[...] = rest_ref[...] * scale + jnp.sum(rest, axis=1, keepdims=True)
    hit_ref[...] = hit_ref[...] * scale + jnp.sum(hit, axis=1, keepdims=True)
    sum_ref[...] = sum_ref[...] * scale + jnp.dot(
        rest.astype(BF16), proj_ref[...], preferred_element_type=F32
    )

    @pl.when(step == pl.num_programs(0) - 1)
    def _():
        out_ref[:, :128] = sum_ref[...]
        lane = lax.broadcasted_iota(jnp.int32, (512, 128), 1)
        stats = jnp.where(lane == 0, max_ref[...], jnp.where(lane == 1, rest_ref[...], hit_ref[...]))
        out_ref[:, 128:] = stats


def merge_kernel(got_ref, rows_ref, out_ref):
    stats = got_ref[:, :, 128:]
    top = jnp.max(stats[:, :, 0:1], axis=0, keepdims=True)
    weight = jnp.exp(stats[:, :, 0:1] - top)
    rest = jnp.sum(weight * stats[:, :, 1:2], axis=0)
    hit = jnp.sum(weight * stats[:, :, 2:3], axis=0)
    total = jnp.sum(weight * got_ref[:, :, :128], axis=0)
    row = jnp.sum(rows_ref[...].astype(F32), axis=0)
    merged = (total - rest * row) / (rest + hit)
    out_ref[...] = jnp.broadcast_to(merged[None], out_ref.shape)


PARAMS = dict(dimension_semantics=("arbitrary",), vmem_limit_bytes=48 << 20)


def head_spec(ref):
    return pl.BlockSpec((ref.shape[0], TILE), lambda i, s: (0, i))


def whole(shape):
    return pl.BlockSpec(shape, lambda i, s: (0,) * len(shape))


def local(hidden_states, head, proj_in, proj_out, targets, lengths):
    z, x, y, c = (lax.axis_index(a) for a in ("z", "x", "y", "c"))
    me = z * 4 + x

    local_target = targets[:, None] - me * 2048
    onehot = (local_target == jnp.arange(2048, dtype=jnp.int32)[None, :]).astype(BF16)
    rows = jnp.dot(onehot, proj_out, preferred_element_type=F32).astype(BF16)
    rows = lax.all_to_all(rows, ("z", "x"), 0, 0, tiled=True).reshape(32, 16, 128)

    stack = gather_hidden(exchange_corners(hidden_states))
    pin = lax.all_gather(proj_in, ("y", "c"), axis=0, tiled=False).reshape(8, 512, 128)

    top, bottom = head[:256], head[256:]
    up_a, down_b = shift(top, "y", 1), shift(bottom, "y", -1)
    up_b, down_a = shift(bottom, "y", 1), shift(top, "y", -1)
    far_a, far_b = shift(up_a, "y", 1), shift(down_b, "y", -1)

    def slot(dy, dc):
        return ((y + dy) % 4) * 2 + (c + dc) % 2

    near = [(head, 0, 0, 512), (up_a, 1, 0, 256), (up_b, 1, 256, 256), (down_a, 2, 0, 256), (down_b, 2, 256, 256)]
    far = [(far_a, 0, 0, 256), (far_b, 0, 256, 256)]

    def both(items, count):
        refs = [i[0] for i in items] + [swap(i[0]) for i in items]
        pieces = [i[1:] for i in items] + [(i[1] + count, i[2], i[3]) for i in items]
        return refs, pieces

    near_refs, near_pieces = both(near, 3)
    far_refs, far_pieces = both(far, 1)
    near_slots = jnp.stack([slot(dy, dc) for dc in (0, 1) for dy in (0, -1, 1)]).astype(jnp.int32)
    far_slots = jnp.stack([slot(2, dc) for dc in (0, 1)]).astype(jnp.int32)

    flops = 2 * 512 * 2048
    part, in_proj = pl.pallas_call(
        functools.partial(first_kernel, near_pieces),
        out_shape=(jax.ShapeDtypeStruct((512, 2048), F32), jax.ShapeDtypeStruct((512, 128), BF16)),
        grid_spec=pltpu.PrefetchScalarGridSpec(
            num_scalar_prefetch=1,
            grid=(2048 // TILE,),
            in_specs=[whole((8, 512, 512)), whole((8, 512, 128))] + [head_spec(r) for r in near_refs],
            out_specs=(pl.BlockSpec((512, TILE), lambda i, s: (0, i)), whole((512, 128))),
        ),
        compiler_params=pltpu.CompilerParams(**PARAMS),
        cost_estimate=pl.CostEstimate(flops=flops * 3072, bytes_accessed=20 << 20, transcendentals=0),
        name="first_slices",
    )(near_slots, stack, pin, *near_refs)

    out = pl.pallas_call(
        functools.partial(last_kernel, far_pieces),
        out_shape=jax.ShapeDtypeStruct((512, 256), F32),
        grid_spec=pltpu.PrefetchScalarGridSpec(
            num_scalar_prefetch=1,
            grid=(2048 // TILE,),
            in_specs=[
                whole((8, 512, 512)),
                pl.BlockSpec((512, TILE), lambda i, s: (0, i)),
                pl.BlockSpec((TILE, 128), lambda i, s: (i, 0)),
                whole((512, 1)),
            ]
            + [head_spec(r) for r in far_refs],
            out_specs=whole((512, 256)),
            scratch_shapes=[pltpu.VMEM((512, 1), F32)] * 3 + [pltpu.VMEM((512, 128), F32)],
        ),
        compiler_params=pltpu.CompilerParams(**PARAMS),
        cost_estimate=pl.CostEstimate(flops=flops * 1152, bytes_accessed=14 << 20, transcendentals=1 << 20),
        name="last_slices",
    )(far_slots, stack, part, proj_out, local_target, *far_refs)

    got = lax.all_to_all(out, ("z", "x"), 0, 0, tiled=True).reshape(32, 16, 256)
    merged = pl.pallas_call(
        merge_kernel,
        out_shape=jax.ShapeDtypeStruct((32, 16, 128), F32),
        name="merge",
    )(got, rows)
    out_proj = lax.all_to_all(merged, ("z", "x"), 0, 0, tiled=True).reshape(512, 128)

    seq_lengths = lengths[0]
    ends = jnp.cumsum(seq_lengths)
    starts = ends - seq_lengths
    positions = jnp.arange(512, dtype=jnp.int32)
    member = (
        (positions[:, None] >= starts[None, :]) & (positions[:, None] < ends[None, :])
    ).astype(F32)
    membership = member / seq_lengths.astype(F32)[None, :]
    in_slice = lax.dynamic_slice_in_dim(in_proj, me * 4, 4, 1)
    expanded = membership[:, :, None] * in_slice.astype(F32)[:, None, :]
    return jnp.einsum("ter,tc->erc", expanded, out_proj, precision=lax.Precision.HIGHEST)


def solution(mesh):
    fine = Mesh(mesh.devices.reshape(8, 4, 4, 2), ("z", "x", "y", "c"))
    tok, voc = ("z", "x"), ("y", "c")
    placed = (P(tok, voc), P(voc, tok), P(voc, None), P(tok, None), P(voc), P(voc, None))
    return jax.shard_map(
        local, mesh=fine, in_specs=placed, out_specs=P(voc, tok, None), check_vma=False
    )
```

```python
import functools

import jax
import jax.numpy as jnp
from jax import lax
from jax.experimental import pallas as pl
from jax.experimental.pallas import tpu as pltpu
from jax.sharding import Mesh, PartitionSpec as P

TILE = 512
FA = 1 << 20
FB = 1 << 20
SLICE = 1 << 36
F32 = jnp.float32
BF16 = jnp.bfloat16


def shift(x, axis, by):
    n = lax.axis_size(axis)
    return lax.ppermute(x, axis, [(i, (i + by) % n) for i in range(n)])


def swap(x):
    return shift(x, "c", 1)


def exchange_corners(x):
    pairs = []
    for z in range(8):
        for xx in range(4):
            for v in range(8):
                src = (z * 4 + xx) * 8 + v
                dst = (v * 4 + xx) * 8 + z
                pairs.append((src, dst))
    return lax.ppermute(x, ("z", "x", "y", "c"), pairs)


def along_x(block):
    x = lax.axis_index("x")
    out = jnp.zeros((512, 512), BF16)
    for by in (0, 1, 3, 2):
        got = block if by == 0 else shift(block, "x", by)
        out = lax.dynamic_update_slice(out, got, (((x - by) % 4) * 128, 0))
    return out


def halves_kernel(up_ref, down_ref, early_ref, a_ref, b_ref):
    a_ref[...] = up_ref[...]
    b_ref[...] = down_ref[...]


def halves(up, down, early):
    half = jax.ShapeDtypeStruct((256, 2048), BF16)
    block = (128, 2048)
    return pl.pallas_call(
        halves_kernel,
        out_shape=(half, half),
        grid=(2,),
        in_specs=[
            pl.BlockSpec(block, lambda i: (i, 0)),
            pl.BlockSpec(block, lambda i: (i + 2, 0)),
            pl.BlockSpec(memory_space=pl.ANY),
        ],
        out_specs=(pl.BlockSpec(block, lambda i: (i, 0)), pl.BlockSpec(block, lambda i: (i, 0))),
        cost_estimate=pl.CostEstimate(flops=SLICE, bytes_accessed=4 << 20, transcendentals=0),
        name="halves",
    )(up, down, early)


def dots(hid_ref, slot_ref, pieces, refs, acc):
    for ref, (place, low, rows) in zip(refs, pieces):
        part = jnp.dot(
            hid_ref[slot_ref[place], :, low : low + rows], ref[...], preferred_element_type=F32
        )
        acc = part if acc is None else acc + part
    return acc


def first_kernel(pieces, slot_ref, hid_ref, *refs):
    heads, part_ref = refs[: len(pieces)], refs[len(pieces)]
    part_ref[...] = dots(hid_ref, slot_ref, pieces, heads, None)


def last_kernel(pieces, slot_ref, hid_ref, part_ref, proj_ref, tgt_ref, rows_ref, *refs):
    heads, (out_ref, max_ref, rest_ref, hit_ref, sum_ref) = refs[: len(pieces)], refs[len(pieces) :]
    step = pl.program_id(0)

    @pl.when(step == 0)
    def _():
        max_ref[...] = jnp.full_like(max_ref, -jnp.inf)
        rest_ref[...] = jnp.zeros_like(rest_ref)
        hit_ref[...] = jnp.zeros_like(hit_ref)
        sum_ref[...] = jnp.zeros_like(sum_ref)

    logits = dots(hid_ref, slot_ref, pieces, heads, part_ref[...])
    old = max_ref[...]
    new = jnp.maximum(old, jnp.max(logits, axis=1, keepdims=True))
    scale = jnp.exp(old - new)
    shifted = jnp.exp(logits - new)
    columns = lax.broadcasted_iota(jnp.int32, logits.shape, 1) + step * TILE
    at_target = columns == tgt_ref[...]
    rest = jnp.where(at_target, 0.0, shifted)
    hit = jnp.where(at_target, shifted, 0.0)
    max_ref[...] = new
    rest_ref[...] = rest_ref[...] * scale + jnp.sum(rest, axis=1, keepdims=True)
    hit_ref[...] = hit_ref[...] * scale + jnp.sum(hit, axis=1, keepdims=True)
    sum_ref[...] = sum_ref[...] * scale + jnp.dot(
        rest.astype(BF16), proj_ref[...], preferred_element_type=F32
    )

    @pl.when(step == pl.num_programs(0) - 1)
    def _():
        out_ref[:, :128] = sum_ref[...].astype(BF16)
        lane = lax.broadcasted_iota(jnp.int32, (512, 128), 1)
        stats = jnp.where(lane < 3, max_ref[...], jnp.where(lane < 6, rest_ref[...], hit_ref[...]))
        high = stats.astype(BF16).astype(F32)
        middle = (stats - high).astype(BF16).astype(F32)
        low = stats - high - middle
        term = lane % 3
        out_ref[:, 256:] = rows_ref[...]
        out_ref[:, 128:256] = jnp.where(term == 0, high, jnp.where(term == 1, middle, low)).astype(BF16)


def merge_kernel(got_ref, out_ref):
    terms = got_ref[:, :, 128:256].astype(F32)
    top, rest, hit = (
        terms[:, :, i : i + 1] + terms[:, :, i + 1 : i + 2] + terms[:, :, i + 2 : i + 3]
        for i in (0, 3, 6)
    )
    weight = jnp.exp(top - jnp.max(top, axis=0, keepdims=True))
    rest = jnp.sum(weight * rest, axis=0)
    hit = jnp.sum(weight * hit, axis=0)
    total = jnp.sum(weight * got_ref[:, :, :128].astype(F32), axis=0)
    row = jnp.sum(got_ref[:, :, 256:].astype(F32), axis=0)
    merged = ((total - rest * row) / (rest + hit)).astype(BF16)
    out_ref[...] = jnp.broadcast_to(merged[None], out_ref.shape)


PARAMS = dict(dimension_semantics=("arbitrary",), vmem_limit_bytes=48 << 20)


def head_spec(ref):
    return pl.BlockSpec((ref.shape[0], TILE), lambda i, s: (0, i))


def whole(shape):
    return pl.BlockSpec(shape, lambda i, s: (0,) * len(shape))


def local(hidden_states, head, proj_in, proj_out, targets, lengths):
    z, x, y, c = (lax.axis_index(a) for a in ("z", "x", "y", "c"))
    me = z * 4 + x

    up, down = shift(head, "y", 1), shift(head, "y", -1)
    pin = lax.all_gather(exchange_corners(proj_in), "z", axis=0, tiled=False)
    mine = along_x(exchange_corners(hidden_states))
    hid = lax.all_gather(mine, "z", axis=0, tiled=False)
    far_a, far_b = halves(up, down, mine)
    far_a, far_b = shift(far_a, "y", 1), shift(far_b, "y", -1)

    local_target = targets[:, None] - me * 2048
    onehot = (local_target == jnp.arange(2048, dtype=jnp.int32)[None, :]).astype(BF16)
    rows = jnp.dot(onehot, proj_out, preferred_element_type=F32).astype(BF16)

    def slot(dy, dc):
        return ((y + dy) % 4) * 2 + (c + dc) % 2

    near = [(head, 0, 0, 512), (up, 1, 0, 512), (down, 2, 0, 512)]
    far = [(far_a, 0, 0, 256), (far_b, 0, 256, 256)]

    def both(items, count):
        refs = [i[0] for i in items] + [swap(i[0]) for i in items]
        pieces = [i[1:] for i in items] + [(i[1] + count, i[2], i[3]) for i in items]
        return refs, pieces

    near_refs, near_pieces = both(near, 3)
    far_refs, far_pieces = both(far, 1)
    near_slots = jnp.stack([slot(dy, dc) for dc in (0, 1) for dy in (0, -1, 1)]).astype(jnp.int32)
    far_slots = jnp.stack([slot(2, dc) for dc in (0, 1)]).astype(jnp.int32)

    part = pl.pallas_call(
        functools.partial(first_kernel, near_pieces),
        out_shape=jax.ShapeDtypeStruct((512, 2048), F32),
        grid_spec=pltpu.PrefetchScalarGridSpec(
            num_scalar_prefetch=1,
            grid=(2048 // TILE,),
            in_specs=[whole((8, 512, 512))] + [head_spec(r) for r in near_refs],
            out_specs=pl.BlockSpec((512, TILE), lambda i, s: (0, i)),
        ),
        compiler_params=pltpu.CompilerParams(**PARAMS),
        cost_estimate=pl.CostEstimate(flops=FA, bytes_accessed=1 << 20, transcendentals=0),
        name="first_slices",
    )(near_slots, hid, *near_refs)

    out = pl.pallas_call(
        functools.partial(last_kernel, far_pieces),
        out_shape=jax.ShapeDtypeStruct((512, 384), BF16),
        grid_spec=pltpu.PrefetchScalarGridSpec(
            num_scalar_prefetch=1,
            grid=(2048 // TILE,),
            in_specs=[
                whole((8, 512, 512)),
                pl.BlockSpec((512, TILE), lambda i, s: (0, i)),
                pl.BlockSpec((TILE, 128), lambda i, s: (i, 0)),
                whole((512, 1)),
                whole((512, 128)),
            ]
            + [head_spec(r) for r in far_refs],
            out_specs=whole((512, 384)),
            scratch_shapes=[pltpu.VMEM((512, 1), F32)] * 3 + [pltpu.VMEM((512, 128), F32)],
        ),
        compiler_params=pltpu.CompilerParams(**PARAMS),
        cost_estimate=pl.CostEstimate(flops=FB, bytes_accessed=1 << 20, transcendentals=0),
        name="last_slices",
    )(far_slots, hid, part, proj_out, local_target, rows, *far_refs)

    got = lax.all_to_all(out, ("z", "x"), 0, 0, tiled=True).reshape(32, 16, 384)
    merged = pl.pallas_call(
        merge_kernel,
        out_shape=jax.ShapeDtypeStruct((32, 16, 128), BF16),
        name="merge",
    )(got)
    out_proj = lax.all_to_all(merged, ("z", "x"), 0, 0, tiled=True).reshape(512, 128).astype(F32)

    seq_lengths = lengths[0]
    ends = jnp.cumsum(seq_lengths)
    starts = ends - seq_lengths
    positions = jnp.arange(512, dtype=jnp.int32)
    member = (
        (positions[:, None] >= starts[None, :]) & (positions[:, None] < ends[None, :])
    ).astype(F32)
    membership = member / seq_lengths.astype(F32)[None, :]
    in_proj = sum(jnp.dot(hid[d], pin[d], preferred_element_type=F32) for d in range(8)).astype(BF16)
    in_slice = lax.dynamic_slice_in_dim(in_proj, me * 4, 4, 1)
    expanded = membership[:, :, None] * in_slice.astype(F32)[:, None, :]
    return jnp.einsum("ter,tc->erc", expanded, out_proj, precision=lax.Precision.HIGHEST)


def solution(mesh):
    fine = Mesh(mesh.devices.reshape(8, 4, 4, 2), ("z", "x", "y", "c"))
    tok, voc = ("z", "x"), ("y", "c")
    placed = (P(tok, voc), P(voc, tok), P(voc, None), P(tok, None), P(voc), P(voc, None))
    return jax.shard_map(
        local, mesh=fine, in_specs=placed, out_specs=P(voc, tok, None), check_vma=False
    )
```

```python
import functools

import jax
import jax.numpy as jnp
from jax import lax
from jax.experimental import pallas as pl
from jax.experimental.pallas import tpu as pltpu
from jax.sharding import Mesh, PartitionSpec as P

TILE = 512
FA = 1 << 20
SLICE = 1 << 36
BLOCK = 1 << 20
F32 = jnp.float32
BF16 = jnp.bfloat16


def shift(x, axis, by):
    n = lax.axis_size(axis)
    return lax.ppermute(x, axis, [(i, (i + by) % n) for i in range(n)])


def swap(x):
    return shift(x, "c", 1)


def exchange_corners(x):
    pairs = []
    for z in range(8):
        for xx in range(4):
            for v in range(8):
                src = (z * 4 + xx) * 8 + v
                dst = (v * 4 + xx) * 8 + z
                pairs.append((src, dst))
    return lax.ppermute(x, ("z", "x", "y", "c"), pairs)


def along_x(block):
    x = lax.axis_index("x")
    out = jnp.zeros((544, 512), BF16)
    for by in (0, 1, 3, 2):
        got = block if by == 0 else shift(block, "x", by)
        out = lax.dynamic_update_slice(out, got, (((x - by) % 4) * 128, 0))
    return out


def block_kernel(x_ref, hidden_ref, proj_in_ref, out_ref):
    row = lax.broadcasted_iota(jnp.int32, (32, 128), 0)
    column = lax.broadcasted_iota(jnp.int32, (32, 128), 1)
    chosen = (column == (row // 4) * 16 + row % 4 + 4 * x_ref[0]).astype(BF16)
    out_ref[:128] = hidden_ref[...]
    out_ref[128:] = lax.dot_general(
        chosen, proj_in_ref[...], (((1,), (1,)), ((), ())), preferred_element_type=F32
    ).astype(BF16)


def with_columns(hidden, proj_in, x):
    return pl.pallas_call(
        block_kernel,
        out_shape=jax.ShapeDtypeStruct((160, 512), BF16),
        in_specs=[pl.BlockSpec(memory_space=pltpu.SMEM)] + [pl.BlockSpec(memory_space=pltpu.VMEM)] * 2,
        out_specs=pl.BlockSpec(memory_space=pltpu.VMEM),
        cost_estimate=pl.CostEstimate(flops=BLOCK, bytes_accessed=1 << 20, transcendentals=0),
        name="block",
    )(x.astype(jnp.int32).reshape(1), hidden, proj_in)


def halves_kernel(up_ref, down_ref, early_ref, a_ref, b_ref):
    a_ref[...] = up_ref[...]
    b_ref[...] = down_ref[...]


def halves(up, down, early):
    half = jax.ShapeDtypeStruct((256, 2048), BF16)
    block = (128, 2048)
    return pl.pallas_call(
        halves_kernel,
        out_shape=(half, half),
        grid=(2,),
        in_specs=[
            pl.BlockSpec(block, lambda i: (i, 0)),
            pl.BlockSpec(block, lambda i: (i + 2, 0)),
            pl.BlockSpec(memory_space=pl.ANY),
        ],
        out_specs=(pl.BlockSpec(block, lambda i: (i, 0)), pl.BlockSpec(block, lambda i: (i, 0))),
        cost_estimate=pl.CostEstimate(flops=SLICE, bytes_accessed=4 << 20, transcendentals=0),
        name="halves",
    )(up, down, early)


def dots(hid_ref, slot_ref, pieces, refs):
    acc = None
    for ref, (place, low, rows) in zip(refs, pieces):
        part = jnp.dot(
            hid_ref[slot_ref[place], :512, low : low + rows], ref[...], preferred_element_type=F32
        )
        acc = part if acc is None else acc + part
    return acc


def head_kernel(pieces, slot_ref, hid_ref, proj_ref, tgt_ref, rows_ref, *refs):
    heads, (out_ref, max_ref, rest_ref, hit_ref, sum_ref) = refs[: len(pieces)], refs[len(pieces) :]
    step = pl.program_id(0)

    @pl.when(step == 0)
    def _():
        max_ref[...] = jnp.full_like(max_ref, -jnp.inf)
        rest_ref[...] = jnp.zeros_like(rest_ref)
        hit_ref[...] = jnp.zeros_like(hit_ref)
        sum_ref[...] = jnp.zeros_like(sum_ref)

    logits = dots(hid_ref, slot_ref, pieces, heads)
    old = max_ref[...]
    new = jnp.maximum(old, jnp.max(logits, axis=1, keepdims=True))
    scale = jnp.exp(old - new)
    shifted = jnp.exp(logits - new)
    columns = lax.broadcasted_iota(jnp.int32, logits.shape, 1) + step * TILE
    at_target = columns == tgt_ref[...]
    rest = jnp.where(at_target, 0.0, shifted)
    hit = jnp.where(at_target, shifted, 0.0)
    max_ref[...] = new
    rest_ref[...] = rest_ref[...] * scale + jnp.sum(rest, axis=1, keepdims=True)
    hit_ref[...] = hit_ref[...] * scale + jnp.sum(hit, axis=1, keepdims=True)
    sum_ref[...] = sum_ref[...] * scale + jnp.dot(
        rest.astype(BF16), proj_ref[...], preferred_element_type=F32
    )

    @pl.when(step == pl.num_programs(0) - 1)
    def _():
        out_ref[:, :128] = sum_ref[...].astype(BF16)
        lane = lax.broadcasted_iota(jnp.int32, (512, 128), 1)
        stats = jnp.where(lane < 3, max_ref[...], jnp.where(lane < 6, rest_ref[...], hit_ref[...]))
        high = stats.astype(BF16).astype(F32)
        middle = (stats - high).astype(BF16).astype(F32)
        low = stats - high - middle
        term = lane % 3
        out_ref[:, 256:] = rows_ref[...]
        out_ref[:, 128:256] = jnp.where(term == 0, high, jnp.where(term == 1, middle, low)).astype(BF16)


def project_kernel(hid_ref, out_ref, sum_ref):
    @pl.when(pl.program_id(0) == 0)
    def _():
        sum_ref[...] = jnp.zeros_like(sum_ref)

    sum_ref[...] += lax.dot_general(
        hid_ref[0, 512:], hid_ref[0, :512], (((1,), (1,)), ((), ())), preferred_element_type=F32
    )
    out_ref[...] = sum_ref[...].astype(BF16)


def merge_kernel(got_ref, out_ref):
    terms = got_ref[:, :, 128:256].astype(F32)
    top, rest, hit = (
        terms[:, :, i : i + 1] + terms[:, :, i + 1 : i + 2] + terms[:, :, i + 2 : i + 3]
        for i in (0, 3, 6)
    )
    weight = jnp.exp(top - jnp.max(top, axis=0, keepdims=True))
    rest = jnp.sum(weight * rest, axis=0)
    hit = jnp.sum(weight * hit, axis=0)
    total = jnp.sum(weight * got_ref[:, :, :128].astype(F32), axis=0)
    row = jnp.sum(got_ref[:, :, 256:].astype(F32), axis=0)
    merged = ((total - rest * row) / (rest + hit)).astype(BF16)
    out_ref[...] = jnp.broadcast_to(merged[None], out_ref.shape)


def final_kernel(lengths_ref, in_ref, rows_ref, out_ref):
    position = lax.broadcasted_iota(jnp.int32, (16, 512), 1)
    columns = in_ref[...]
    start = 0
    masked = []
    for e in range(8):
        end = start + lengths_ref[0, e]
        inside = jnp.logical_and(position >= start, position < end)
        masked.append(jnp.where(inside, columns, jnp.zeros_like(columns)))
        start = end
    summed = jnp.dot(jnp.concatenate(masked, axis=0), rows_ref[...], preferred_element_type=F32)
    for e in range(8):
        length = jnp.full((4, 128), lengths_ref[0, e], jnp.int32).astype(F32)
        out_ref[e] = summed[16 * e : 16 * e + 4] / length


PARAMS = dict(dimension_semantics=("arbitrary",), vmem_limit_bytes=48 << 20)


def head_spec(ref):
    return pl.BlockSpec((ref.shape[0], TILE), lambda i, s: (0, i))


def whole(shape):
    return pl.BlockSpec(shape, lambda i, s: (0,) * len(shape))


def local(hidden_states, head, proj_in, proj_out, targets, lengths):
    z, x, y, c = (lax.axis_index(a) for a in ("z", "x", "y", "c"))
    me = z * 4 + x

    up, down = shift(head, "y", 1), shift(head, "y", -1)
    block = exchange_corners(with_columns(hidden_states, proj_in, x))
    mine = lax.dynamic_update_slice(along_x(block[:128]), block[128:], (512, 0))
    hid = lax.all_gather(mine, "z", axis=0, tiled=False)
    far_a, far_b = halves(up, down, block)
    far_a, far_b = shift(far_a, "y", 1), shift(far_b, "y", -1)

    local_target = targets[:, None] - me * 2048
    onehot = (local_target == jnp.arange(2048, dtype=jnp.int32)[None, :]).astype(BF16)
    rows = jnp.dot(onehot, proj_out, preferred_element_type=F32).astype(BF16)

    def slot(dy, dc):
        return ((y + dy) % 4) * 2 + (c + dc) % 2

    items = [(head, 0, 0, 512), (up, 1, 0, 512), (down, 2, 0, 512)]
    items += [(far_a, 3, 0, 256), (far_b, 3, 256, 256)]
    refs = [i[0] for i in items] + [swap(i[0]) for i in items]
    pieces = [i[1:] for i in items] + [(i[1] + 4, i[2], i[3]) for i in items]
    slots = jnp.stack([slot(dy, dc) for dc in (0, 1) for dy in (0, -1, 1, 2)]).astype(jnp.int32)

    out = pl.pallas_call(
        functools.partial(head_kernel, pieces),
        out_shape=jax.ShapeDtypeStruct((512, 384), BF16),
        grid_spec=pltpu.PrefetchScalarGridSpec(
            num_scalar_prefetch=1,
            grid=(2048 // TILE,),
            in_specs=[
                whole((8, 544, 512)),
                pl.BlockSpec((TILE, 128), lambda i, s: (i, 0)),
                whole((512, 1)),
                whole((512, 128)),
            ]
            + [head_spec(r) for r in refs],
            out_specs=whole((512, 384)),
            scratch_shapes=[pltpu.VMEM((512, 1), F32)] * 3 + [pltpu.VMEM((512, 128), F32)],
        ),
        compiler_params=pltpu.CompilerParams(**PARAMS),
        cost_estimate=pl.CostEstimate(flops=FA, bytes_accessed=1 << 20, transcendentals=0),
        name="head",
    )(slots, hid, proj_out, local_target, rows, *refs)

    got = lax.all_to_all(out, ("z", "x"), 0, 0, tiled=True).reshape(32, 16, 384)
    in_proj = pl.pallas_call(
        project_kernel,
        out_shape=jax.ShapeDtypeStruct((32, 512), BF16),
        grid=(8,),
        in_specs=[
            pl.BlockSpec((1, 544, 512), lambda i: (i, 0, 0)),
        ],
        out_specs=pl.BlockSpec((32, 512), lambda i: (0, 0)),
        scratch_shapes=[pltpu.VMEM((32, 512), F32)],
        cost_estimate=pl.CostEstimate(flops=1 << 30, bytes_accessed=4 << 20, transcendentals=0),
        name="project",
    )(hid)
    in_proj = lax.dynamic_slice_in_dim(in_proj, 4 * z, 4, 0)
    in_proj = jnp.concatenate([in_proj, jnp.zeros((12, 512), BF16)], axis=0)
    in_vmem = pl.BlockSpec(memory_space=pltpu.VMEM)
    merged = pl.pallas_call(
        merge_kernel,
        out_shape=jax.ShapeDtypeStruct((32, 16, 128), BF16),
        in_specs=[in_vmem],
        out_specs=in_vmem,
        name="merge",
    )(got)
    out_proj = lax.all_to_all(merged, ("z", "x"), 0, 0, tiled=True).reshape(512, 128)
    return pl.pallas_call(
        final_kernel,
        out_shape=jax.ShapeDtypeStruct((8, 4, 128), F32),
        in_specs=[pl.BlockSpec(memory_space=pltpu.SMEM), in_vmem, in_vmem],
        out_specs=in_vmem,
        name="final",
    )(lengths, in_proj, out_proj)


def solution(mesh):
    fine = Mesh(mesh.devices.reshape(8, 4, 4, 2), ("z", "x", "y", "c"))
    tok, voc = ("z", "x"), ("y", "c")
    placed = (P(tok, voc), P(voc, tok), P(voc, None), P(tok, None), P(voc), P(voc, None))
    return jax.shard_map(
        local, mesh=fine, in_specs=placed, out_specs=P(voc, tok, None), check_vma=False
    )
```

```python
import functools

import jax
import jax.numpy as jnp
from jax import lax
from jax.experimental import pallas as pl
from jax.experimental.pallas import tpu as pltpu
from jax.sharding import Mesh, PartitionSpec as P

TILE = 512
FA = 1 << 20
SLICE = 1 << 33
BLOCK = 1 << 20
F32 = jnp.float32
BF16 = jnp.bfloat16


def shift(x, axis, by):
    n = lax.axis_size(axis)
    return lax.ppermute(x, axis, [(i, (i + by) % n) for i in range(n)])


def swap(x):
    return shift(x, "c", 1)


def exchange_corners(x):
    pairs = []
    for z in range(8):
        for xx in range(4):
            for v in range(8):
                src = (z * 4 + xx) * 8 + v
                dst = (v * 4 + xx) * 8 + z
                pairs.append((src, dst))
    return lax.ppermute(x, ("z", "x", "y", "c"), pairs)


def along_x(block):
    x = lax.axis_index("x")
    out = jnp.zeros((544, 512), BF16)
    for by in (0, 1, 3, 2):
        got = block if by == 0 else shift(block, "x", by)
        out = lax.dynamic_update_slice(out, got, (((x - by) % 4) * 128, 0))
    return out


def ring_z(block, before_third):
    half = block.shape[0] // 2
    right, left = [block], [block]
    for step in range(3):
        sent = (right[-1], left[-1])
        if step == 2:
            sent, before_third = lax.optimization_barrier((sent, before_third))
        right.append(shift(sent[0], "z", 1))
        left.append(shift(sent[1], "z", -1))
    far = [shift(right[-1][:half], "z", 1), shift(left[-1][half:], "z", -1)]
    return right + far + left[:0:-1], before_third


def load_hidden(block_refs, hid_ref, sems):
    half = hid_ref.shape[1] // 2
    places = [hid_ref.at[i] for i in range(4)]
    places += [hid_ref.at[4, pl.ds(0, half)], hid_ref.at[4, pl.ds(half, half)]]
    places += [hid_ref.at[i] for i in range(5, 8)]
    copies = [
        pltpu.make_async_copy(ref, place, sems.at[i])
        for i, (ref, place) in enumerate(zip(block_refs, places))
    ]
    for copy in copies:
        copy.start()
    for copy in copies:
        copy.wait()


def block_kernel(x_ref, hidden_ref, proj_in_ref, out_ref):
    row = lax.broadcasted_iota(jnp.int32, (32, 128), 0)
    column = lax.broadcasted_iota(jnp.int32, (32, 128), 1)
    chosen = (column == (row // 4) * 16 + row % 4 + 4 * x_ref[0]).astype(BF16)
    out_ref[:128] = hidden_ref[...]
    out_ref[128:] = lax.dot_general(
        chosen, proj_in_ref[...], (((1,), (1,)), ((), ())), preferred_element_type=F32
    ).astype(BF16)


def with_columns(hidden, proj_in, x):
    return pl.pallas_call(
        block_kernel,
        out_shape=jax.ShapeDtypeStruct((160, 512), BF16),
        in_specs=[pl.BlockSpec(memory_space=pltpu.SMEM)] + [pl.BlockSpec(memory_space=pltpu.VMEM)] * 2,
        out_specs=pl.BlockSpec(memory_space=pltpu.VMEM),
        cost_estimate=pl.CostEstimate(flops=BLOCK, bytes_accessed=1 << 20, transcendentals=0),
        name="block",
    )(x.astype(jnp.int32).reshape(1), hidden, proj_in)


def halves_kernel(up_ref, down_ref, early_ref, a_ref, b_ref):
    a_ref[...] = up_ref[...]
    b_ref[...] = down_ref[...]


def halves(up, down, early):
    half = jax.ShapeDtypeStruct((256, 2048), BF16)
    block = (128, 2048)
    return pl.pallas_call(
        halves_kernel,
        out_shape=(half, half),
        grid=(2,),
        in_specs=[
            pl.BlockSpec(block, lambda i: (i, 0)),
            pl.BlockSpec(block, lambda i: (i + 2, 0)),
            pl.BlockSpec(memory_space=pl.ANY),
        ],
        out_specs=(pl.BlockSpec(block, lambda i: (i, 0)), pl.BlockSpec(block, lambda i: (i, 0))),
        cost_estimate=pl.CostEstimate(flops=SLICE, bytes_accessed=4 << 20, transcendentals=0),
        name="halves",
    )(up, down, early)


def dots(hid_ref, slot_ref, pieces, refs):
    acc = None
    for ref, (place, low, rows) in zip(refs, pieces):
        part = jnp.dot(
            hid_ref[slot_ref[place], :512, low : low + rows], ref[...], preferred_element_type=F32
        )
        acc = part if acc is None else acc + part
    return acc


def head_kernel(pieces, slot_ref, *refs):
    blocks, (proj_ref, tgt_ref, rows_ref), heads = refs[:9], refs[9:12], refs[12 : 12 + len(pieces)]
    out_ref, max_ref, rest_ref, hit_ref, sum_ref, hid_ref, sems = refs[12 + len(pieces) :]
    step = pl.program_id(0)

    @pl.when(step == 0)
    def _():
        load_hidden(blocks, hid_ref, sems)
        max_ref[...] = jnp.full_like(max_ref, -jnp.inf)
        rest_ref[...] = jnp.zeros_like(rest_ref)
        hit_ref[...] = jnp.zeros_like(hit_ref)
        sum_ref[...] = jnp.zeros_like(sum_ref)

    logits = dots(hid_ref, slot_ref, pieces, heads)
    old = max_ref[...]
    new = jnp.maximum(old, jnp.max(logits, axis=1, keepdims=True))
    scale = jnp.exp(old - new)
    shifted = jnp.exp(logits - new)
    columns = lax.broadcasted_iota(jnp.int32, logits.shape, 1) + step * TILE
    at_target = columns == tgt_ref[...]
    rest = jnp.where(at_target, 0.0, shifted)
    hit = jnp.where(at_target, shifted, 0.0)
    max_ref[...] = new
    rest_ref[...] = rest_ref[...] * scale + jnp.sum(rest, axis=1, keepdims=True)
    hit_ref[...] = hit_ref[...] * scale + jnp.sum(hit, axis=1, keepdims=True)
    sum_ref[...] = sum_ref[...] * scale + jnp.dot(
        rest.astype(BF16), proj_ref[...], preferred_element_type=F32
    )

    @pl.when(step == pl.num_programs(0) - 1)
    def _():
        out_ref[:, :128] = sum_ref[...].astype(BF16)
        lane = lax.broadcasted_iota(jnp.int32, (512, 128), 1)
        stats = jnp.where(lane < 3, max_ref[...], jnp.where(lane < 6, rest_ref[...], hit_ref[...]))
        high = stats.astype(BF16).astype(F32)
        middle = (stats - high).astype(BF16).astype(F32)
        low = stats - high - middle
        term = lane % 3
        out_ref[:, 256:] = rows_ref[...]
        out_ref[:, 128:256] = jnp.where(term == 0, high, jnp.where(term == 1, middle, low)).astype(BF16)


def project_kernel(*refs):
    out_ref, hid_ref, sems = refs[9:]
    load_hidden(refs[:9], hid_ref, sems)
    total = jnp.zeros((32, 512), F32)
    for i in range(8):
        total = total + lax.dot_general(
            hid_ref[i, 512:], hid_ref[i, :512], (((1,), (1,)), ((), ())), preferred_element_type=F32
        )
    out_ref[...] = total.astype(BF16)


def merge_kernel(got_ref, out_ref):
    terms = got_ref[:, :, 128:256].astype(F32)
    top, rest, hit = (
        terms[:, :, i : i + 1] + terms[:, :, i + 1 : i + 2] + terms[:, :, i + 2 : i + 3]
        for i in (0, 3, 6)
    )
    weight = jnp.exp(top - jnp.max(top, axis=0, keepdims=True))
    rest = jnp.sum(weight * rest, axis=0)
    hit = jnp.sum(weight * hit, axis=0)
    total = jnp.sum(weight * got_ref[:, :, :128].astype(F32), axis=0)
    row = jnp.sum(got_ref[:, :, 256:].astype(F32), axis=0)
    merged = ((total - rest * row) / (rest + hit)).astype(BF16)
    out_ref[...] = jnp.broadcast_to(merged[None], out_ref.shape)


def final_kernel(lengths_ref, in_ref, rows_ref, out_ref):
    position = lax.broadcasted_iota(jnp.int32, (16, 512), 1)
    columns = in_ref[...]
    start = 0
    masked = []
    for e in range(8):
        end = start + lengths_ref[0, e]
        inside = jnp.logical_and(position >= start, position < end)
        masked.append(jnp.where(inside, columns, jnp.zeros_like(columns)))
        start = end
    summed = jnp.dot(jnp.concatenate(masked, axis=0), rows_ref[...], preferred_element_type=F32)
    for e in range(8):
        length = jnp.full((4, 128), lengths_ref[0, e], jnp.int32).astype(F32)
        out_ref[e] = summed[16 * e : 16 * e + 4] / length


PARAMS = dict(dimension_semantics=("arbitrary",), vmem_limit_bytes=60 << 20)


def head_spec(ref):
    return pl.BlockSpec((ref.shape[0], TILE), lambda i, s: (0, i))


def whole(shape):
    return pl.BlockSpec(shape, lambda i, s: (0,) * len(shape))


def local(hidden_states, head, proj_in, proj_out, targets, lengths):
    z, x, y, c = (lax.axis_index(a) for a in ("z", "x", "y", "c"))
    me = z * 4 + x

    up, down = shift(head, "y", 1), shift(head, "y", -1)
    head_swapped = swap(head)
    hidden_states, head_swapped = lax.optimization_barrier((hidden_states, head_swapped))
    block = exchange_corners(with_columns(hidden_states, proj_in, x))
    mine = lax.dynamic_update_slice(along_x(block[:128]), block[128:], (512, 0))
    hid, (far_a, far_b) = ring_z(mine, halves(up, down, block))
    far_a, far_b = shift(far_a, "y", 1), shift(far_b, "y", -1)

    local_target = targets[:, None] - me * 2048
    onehot = (local_target == jnp.arange(2048, dtype=jnp.int32)[None, :]).astype(BF16)
    rows = jnp.dot(onehot, proj_out, preferred_element_type=F32).astype(BF16)

    def slot(dy, dc):
        return ((y + dy) % 4) * 2 + (c + dc) % 2

    items = [(head, 0, 0, 512), (up, 1, 0, 512), (down, 2, 0, 512)]
    items += [(far_a, 3, 0, 256), (far_b, 3, 256, 256)]
    refs = [i[0] for i in items]
    near_later, _ = lax.optimization_barrier((refs[1:3], hid[2]))
    pieces = [i[1:] for i in items] + [(i[1] + 4, i[2], i[3]) for i in items]
    slots = jnp.stack([slot(dy, dc) for dc in (0, 1) for dy in (0, -1, 1, 2)])
    slots = ((z - slots) % 8).astype(jnp.int32)

    far_later, _, rows, local_target, slots = lax.optimization_barrier(
        (refs[3:], (hid[4], hid[5]), rows, local_target, slots)
    )
    refs += [head_swapped] + [swap(r) for r in near_later + far_later]
    out = pl.pallas_call(
        functools.partial(head_kernel, pieces),
        out_shape=jax.ShapeDtypeStruct((512, 384), BF16),
        grid_spec=pltpu.PrefetchScalarGridSpec(
            num_scalar_prefetch=1,
            grid=(2048 // TILE,),
            in_specs=[
                *[pl.BlockSpec(memory_space=pl.ANY)] * 9,
                pl.BlockSpec((TILE, 128), lambda i, s: (i, 0)),
                whole((512, 1)),
                whole((512, 128)),
            ]
            + [head_spec(r) for r in refs],
            out_specs=whole((512, 384)),
            scratch_shapes=[pltpu.VMEM((512, 1), F32)] * 3
            + [pltpu.VMEM((512, 128), F32), pltpu.VMEM((8, 544, 512), BF16)]
            + [pltpu.SemaphoreType.DMA((9,))],
        ),
        compiler_params=pltpu.CompilerParams(**PARAMS),
        cost_estimate=pl.CostEstimate(flops=FA, bytes_accessed=1 << 20, transcendentals=0),
        name="head",
    )(slots, *hid, proj_out, local_target, rows, *refs)

    got = lax.all_to_all(out, ("z", "x"), 0, 0, tiled=True).reshape(32, 16, 384)
    in_proj = pl.pallas_call(
        project_kernel,
        out_shape=jax.ShapeDtypeStruct((32, 512), BF16),
        in_specs=[pl.BlockSpec(memory_space=pl.ANY)] * 9,
        scratch_shapes=[pltpu.VMEM((8, 544, 512), BF16), pltpu.SemaphoreType.DMA((9,))],
        compiler_params=pltpu.CompilerParams(vmem_limit_bytes=48 << 20),
        cost_estimate=pl.CostEstimate(flops=1 << 30, bytes_accessed=4 << 20, transcendentals=0),
        name="project",
    )(*hid)
    in_proj = lax.dynamic_slice_in_dim(in_proj, 4 * z, 4, 0)
    in_proj = jnp.concatenate([in_proj, jnp.zeros((12, 512), BF16)], axis=0)
    in_vmem = pl.BlockSpec(memory_space=pltpu.VMEM)
    merged = pl.pallas_call(
        merge_kernel,
        out_shape=jax.ShapeDtypeStruct((32, 16, 128), BF16),
        in_specs=[in_vmem],
        out_specs=in_vmem,
        name="merge",
    )(got)
    out_proj = lax.all_to_all(merged, ("z", "x"), 0, 0, tiled=True).reshape(512, 128)
    return pl.pallas_call(
        final_kernel,
        out_shape=jax.ShapeDtypeStruct((8, 4, 128), F32),
        in_specs=[pl.BlockSpec(memory_space=pltpu.SMEM), in_vmem, in_vmem],
        out_specs=in_vmem,
        name="final",
    )(lengths, in_proj, out_proj)


def solution(mesh):
    fine = Mesh(mesh.devices.reshape(8, 4, 4, 2), ("z", "x", "y", "c"))
    tok, voc = ("z", "x"), ("y", "c")
    placed = (P(tok, voc), P(voc, tok), P(voc, None), P(tok, None), P(voc), P(voc, None))
    return jax.shard_map(
        local, mesh=fine, in_specs=placed, out_specs=P(voc, tok, None), check_vma=False
    )
```
